32 devices in a mesh: occ: 4 (over x, core), vir: 8 (over z, y).
Axes of the slice: x: 2, y: 2, z: 4, core: 2. Of those that a mesh axis runs over, the one named last changes fastest.
Arguments:
- amplitudes: bfloat16 [8, 1024, 8, 1024], P(None, 'vir', 'occ'), may hold values from -0.0625 to 0.0625
- integrals: bfloat16 [8, 1024, 8, 1024], P(None, 'vir', 'occ'), may hold values from -6 to 6
- occ_irrep: int32 [8], replicated, may hold values from 0 to 1
- tile_irrep: int32 [8], replicated, may hold values from 0 to 1
Outputs:
- cycle_term: bfloat16 [8, 1024, 8, 1024], P('occ', 'vir')
The draws below stay inside these ranges and needn't reach their ends.
Inputs may be any that keep to these rules, and one draw needn't show every extreme that they name: `occ_irrep`: irreps numbered as in D2h, so that the irrep of a product is the exclusive or of the numbers; the orbitals span the irreps 0 and 1. `tile_irrep`: irreps numbered as for occ_irrep.
All inputs are finite; a program needn't handle non-finite values.
Results may differ from the reference program's by a relative error of at most 0.001.
Values may be sent and summed in bfloat16 or wider, within the bound.
No kernel may reach another device: no remote copies, remote signals or barrier semaphores. Data moves between devices by JAX's collectives and lax.ppermute only.
A program may use at most 128 MiB of HBM per device.

```python
import jax
import jax.numpy as jnp
from jax import lax

O = 8
NV = 1024
TILE = 128
NT = 8


def set_ends(drawn, stream_key, smallest, top_value):
    longest = drawn.shape.index(max(drawn.shape))
    spots = []
    for shift in (0, 1):
        where = [jax.random.randint(jax.random.fold_in(stream_key, axis), (), 0, length) for axis, length in enumerate(drawn.shape)]
        where[longest] = (where[longest] + shift) % drawn.shape[longest]
        spots.append(tuple(where))
    return drawn.at[spots[0]].set(smallest).at[spots[1]].set(top_value)


def shard_levels(own_key, dims, pieces, least, largest):
    def one(dim, parts):
        heights = jax.random.uniform(jax.random.fold_in(jax.random.fold_in(own_key, 6), dim), (parts,), jnp.float32, least / len(pieces), largest / len(pieces))
        return jnp.repeat(jnp.exp(heights), dims[dim] // parts).reshape((-1,) + (1,) * (len(dims) - dim - 1))

    level = one(*pieces[0])
    for cut in pieces[1:]:
        level = level * one(*cut)
    return level


def scatter_about(key, shape, width, reach, shards=(), held_as=jnp.bfloat16):
    array = jax.random.normal(key, shape, jnp.float32) * width
    if len(shards) > 0:
        array = shard_levels(key, shape, shards, -0.22, 0.18) * array
    return jnp.clip(array, min=-reach, max=reach).astype(held_as)


def setup_inputs(seed: int = 0) -> dict:
    keys = jax.random.split(jax.random.key(seed), 5)
    return {
        "amplitudes": scatter_about(keys[0], (O, NV, O, NV), (O * NV) ** -0.5, 0.0625, ((1, 8), (2, 4))),
        "integrals": scatter_about(keys[1], (O, NV, O, NV), 1.0, 6.0, ((1, 8), (2, 4))),
        "occ_irrep": set_ends(jax.random.randint(keys[2], (O,), 0, 2), jax.random.fold_in(keys[2], 1), 0, 1).astype(jnp.int32),
        "tile_irrep": set_ends(jax.random.randint(keys[3], (NT,), 0, 2), jax.random.fold_in(keys[3], 1), 0, 1).astype(jnp.int32),
    }


def reference(amplitudes, integrals, occ_irrep, tile_irrep):
    flat_size = O * NV
    tile_codes = tile_irrep[(jnp.arange(NV) // TILE).astype(jnp.int32)]
    pair_code = jnp.bitwise_xor(occ_irrep[:, None], tile_codes[None, :]).reshape(flat_size)
    allowed = pair_code[:, None] == pair_code[None, :]
    flat_amplitudes = amplitudes.reshape(flat_size, flat_size)
    flat_integrals = integrals.reshape(flat_size, flat_size)
    flat_amplitudes = jnp.where(allowed, flat_amplitudes, jnp.zeros_like(flat_amplitudes))
    flat_integrals = jnp.where(allowed, flat_integrals, jnp.zeros_like(flat_integrals))
    contracted = lax.dot_general(flat_amplitudes, flat_integrals, (((1,), (1,)), ((), ())), preferred_element_type=jnp.float32)
    combined = contracted + contracted.T
    return combined.astype(jnp.bfloat16).reshape(O, NV, O, NV)
```

```python
import functools

import jax
import jax.numpy as jnp
from jax import lax
from jax.experimental import pallas as pl
from jax.experimental.pallas import tpu as pltpu
from jax.sharding import PartitionSpec as P

TILE = 128
F32 = jnp.float32
BF16 = jnp.bfloat16
VMEM_LIMIT = 48 * 1024 * 1024
SMEM_SPEC = pl.BlockSpec(memory_space=pltpu.SMEM)
VMEM_SPEC = pl.BlockSpec(memory_space=pltpu.VMEM)


def lookup(values, positions):
    hits = positions[:, None] == jnp.arange(values.shape[0], dtype=jnp.int32)[None, :]
    return jnp.sum(jnp.where(hits, values[None, :], 0), axis=1)


def pair_codes(occ_irrep, tile_irrep, occ_rows, virt_rows):
    return jnp.bitwise_xor(
        lookup(occ_irrep, occ_rows)[:, None], lookup(tile_irrep, virt_rows // TILE)[None, :]
    )


def general_body(amplitudes, integrals, occ_irrep, tile_irrep):
    occ_total, vir_local, sum_local, virt_width = amplitudes.shape
    occ_index = lax.axis_index("occ")
    vir_index = lax.axis_index("vir")
    all_occ = jnp.arange(occ_total, dtype=jnp.int32)
    all_virt = jnp.arange(virt_width, dtype=jnp.int32)
    vir_rows = vir_index * vir_local + jnp.arange(vir_local, dtype=jnp.int32)
    sum_rows = occ_index * sum_local + jnp.arange(sum_local, dtype=jnp.int32)
    left_code = pair_codes(occ_irrep, tile_irrep, all_occ, vir_rows)
    right_code = pair_codes(occ_irrep, tile_irrep, sum_rows, all_virt)
    keep = left_code[:, :, None, None] == right_code[None, None, :, :]
    amplitudes = jnp.where(keep, amplitudes, jnp.zeros_like(amplitudes))
    integrals = jnp.where(keep, integrals, jnp.zeros_like(integrals))
    flat_amplitudes = amplitudes.reshape(occ_total * vir_local, sum_local * virt_width)
    shards = lax.all_gather(integrals, "vir", axis=1, tiled=True)
    block_count = shards.shape[1]
    shard_rows = shards.reshape(occ_total * block_count, sum_local * virt_width)
    product = lax.dot_general(
        flat_amplitudes, shard_rows, (((1,), (1,)), ((), ())), preferred_element_type=jnp.float32
    )
    partial_value = product.reshape(occ_total, vir_local, occ_total, block_count)
    summed = lax.psum_scatter(partial_value, "occ", scatter_dimension=0, tiled=True)
    mirrored = lax.all_to_all(
        lax.all_to_all(summed, "vir", split_axis=3, concat_axis=1, tiled=True),
        "occ",
        split_axis=2,
        concat_axis=0,
        tiled=True,
    )
    combined = summed + jnp.transpose(mirrored, (2, 3, 0, 1))
    return combined.astype(jnp.bfloat16)


def start(size, unit):
    return pl.multiple_of(size * unit, unit)


def pack_kernel(meta, occ, tile, w_ref, out_ref):
    sum_local, rows, width = w_ref.shape
    cts = width // TILE
    own = tile[meta[1]]

    def one(m, n):
        j, k, c = m // (sum_local * cts), (m // cts) % sum_local, m % cts
        ok = (occ[j] ^ own ^ occ[meta[0] * sum_local + k] ^ tile[c]) == 0

        @pl.when(ok)
        def _():
            out_ref[n] = w_ref[k, pl.ds(start(j, TILE), TILE), pl.ds(start(c, TILE), TILE)]

        return n + ok.astype(jnp.int32)

    lax.fori_loop(0, (rows // TILE) * sum_local * cts, one, jnp.int32(0))


def unpack(meta, occ, tile, their, pieces, wd):
    sum_local, rows, width = wd.shape
    cts = width // TILE
    half = pieces[0].shape[0]

    def one(m, n):
        j, k, c = m // (sum_local * cts), (m // cts) % sum_local, m % cts
        ok = (occ[j] ^ their ^ occ[meta[0] * sum_local + k] ^ tile[c]) == 0
        where = (k, pl.ds(start(j, TILE), TILE), pl.ds(start(c, TILE), TILE))
        if len(pieces) == 1:

            @pl.when(ok)
            def _():
                wd[where] = pieces[0][n]
        else:

            @pl.when(ok & (n < half))
            def _():
                wd[where] = pieces[0][n]

            @pl.when(ok & (n >= half))
            def _():
                wd[where] = pieces[1][n - half]

        @pl.when(jnp.logical_not(ok))
        def _():
            wd[where] = jnp.zeros((TILE, TILE), wd.dtype)

        return n + ok.astype(jnp.int32)

    lax.fori_loop(0, (rows // TILE) * sum_local * cts, one, jnp.int32(0))


def products(a_ref, b_ref, rows):
    total = None
    for k in range(a_ref.shape[0]):
        part = lax.dot_general(
            a_ref[k, rows, :], b_ref[k], (((1,), (1,)), ((), ())), preferred_element_type=F32
        )
        total = part if total is None else total + part
    return total


def block_kernel(modes, pieces, owners, slots, meta, occ, tile, t_ref, *refs):
    count = len(modes) * pieces
    w_refs, (keep_ref, send_ref, wd, blk) = refs[:count], refs[count:]
    me = meta[0]
    occ_total = t_ref.shape[1] // TILE
    own_rows = occ_total // owners
    span = own_rows * TILE
    for place, mode in enumerate(modes):
        their = tile[meta[3 + place]]
        same = tile[meta[1]] ^ their
        unpack(meta, occ, tile, their, w_refs[place * pieces : (place + 1) * pieces], wd)

        def share(s, carry, mode=mode, same=same, place=place):
            rows = pl.ds(start(s, span), span)
            if mode == "lead":
                blk[...] = products(t_ref, wd, rows)
            elif mode == "follow":
                blk[...] = products(wd, t_ref, rows)
            elif mode == "self":
                blk[...] = products(t_ref, wd, rows) + products(wd, t_ref, rows)
            else:

                @pl.when(meta[2] == 1)
                def _():
                    blk[...] = products(t_ref, wd, rows)

                @pl.when(meta[2] != 1)
                def _():
                    blk[...] = products(wd, t_ref, rows)

            other = s ^ me
            far, near = other // 2, other % 2

            def one(e, n):
                ii, j = e // occ_total, e % occ_total
                ok = (occ[s * own_rows + ii] ^ occ[j] ^ same) == 0
                part = (pl.ds(start(ii, TILE), TILE), pl.ds(start(j, TILE), TILE))

                @pl.when(ok & (near == 0))
                def _():
                    keep_ref[far, n] = blk[part]

                @pl.when(ok & (near == 1))
                def _():
                    send_ref[far, n] = blk[part]

                return n + ok.astype(jnp.int32)

            lax.fori_loop(0, own_rows * occ_total, one, jnp.int32(place * slots))
            return carry

        lax.fori_loop(0, owners, share, 0)


def mirror_kernel(meta, occ, tile, list_ref, *out_refs):
    owners = len(out_refs)
    own_rows = out_refs[0].shape[0]
    occ_total = owners * own_rows
    me = meta[0]
    same = tile[meta[1]] ^ tile[meta[3]]

    def one(e, n):
        ii, j = e // occ_total, e % occ_total
        ok = (occ[me * own_rows + ii] ^ occ[j] ^ same) == 0
        rel = (j // own_rows) ^ me
        block = list_ref[jnp.minimum(n, list_ref.shape[0] - 1)].astype(F32).T.astype(BF16)
        block = jnp.where(ok, block, jnp.zeros_like(block))
        for q in range(owners):

            @pl.when(rel == q)
            def _(q=q):
                out_refs[q][j % own_rows, ii] = block

        return n + ok.astype(jnp.int32)

    lax.fori_loop(0, own_rows * occ_total, one, jnp.int32(0))


def place_kernel(steps, half, owners, meta, occ, tile, *refs):
    lists = refs[: steps + 1]
    mirrored = refs[steps + 1 : -1]
    out_ref = refs[-1]
    own_rows, occ_total = out_ref.shape[:2]
    me = meta[0]

    def spread(list_ref, partner):
        same = tile[meta[1]] ^ tile[partner]
        cols = pl.ds(start(partner, TILE), TILE)

        def one(e, n):
            ii, j = e // occ_total, e % occ_total
            ok = (occ[me * own_rows + ii] ^ occ[j] ^ same) == 0

            @pl.when(ok)
            def _():
                out_ref[ii, j, :, cols] = list_ref[n].astype(BF16)

            @pl.when(jnp.logical_not(ok))
            def _():
                out_ref[ii, j, :, cols] = jnp.zeros((TILE, TILE), BF16)

            return n + ok.astype(jnp.int32)

        lax.fori_loop(0, own_rows * occ_total, one, jnp.int32(0))

    def lay(blocks, partner):
        cols = pl.ds(start(partner, TILE), TILE)
        for q in range(owners):
            for jj in range(own_rows):
                for ii in range(own_rows):
                    out_ref[jj, (me ^ q) * own_rows + ii, :, cols] = blocks[q][jj, ii]

    spread(lists[0], meta[1])
    for t in range(1, steps + 1):
        theirs = mirrored[(t - 1) * owners : t * owners]
        if t == half:

            @pl.when(meta[2] == 1)
            def _(t=t):
                spread(lists[t], meta[2 + t])

            @pl.when(meta[2] != 1)
            def _(t=t, theirs=theirs):
                lay(theirs, meta[2 + steps + t])
        else:
            spread(lists[t], meta[2 + t])
            lay(theirs, meta[2 + steps + t])


def call(kernel, shapes, scalars, arrays, scratch=(), flops=0):
    moved = sum(a.size * a.dtype.itemsize for a in arrays)
    return pl.pallas_call(
        kernel,
        out_shape=shapes,
        in_specs=[SMEM_SPEC] * len(scalars) + [VMEM_SPEC] * len(arrays),
        out_specs=jax.tree.map(lambda _: VMEM_SPEC, shapes),
        scratch_shapes=list(scratch),
        compiler_params=pltpu.CompilerParams(vmem_limit_bytes=VMEM_LIMIT),
        cost_estimate=pl.CostEstimate(flops=flops, bytes_accessed=2 * moved, transcendentals=0),
    )(*scalars, *arrays)


def ring_body(owners, size, cap, slots, t_rows, w_rows, occ_irrep, tile_irrep):
    sum_local, rows, width = t_rows.shape
    occ_total = rows // TILE
    own_rows = occ_total // owners
    half = size // 2
    order = list(range(0, size, 2)) + list(range(size - 1, 0, -2))
    ring = jnp.array(order, jnp.int32)
    at = [order.index(v) for v in range(size)]
    occ_index = lax.axis_index("occ").astype(jnp.int32)
    vir_index = lax.axis_index("vir").astype(jnp.int32)
    where = jnp.array(at, jnp.int32)[vir_index]
    leads = (where < half).astype(jnp.int32)

    def partner(shift):
        return ring[(where + shift) % size]

    def meta(*more):
        return jnp.stack([occ_index, vir_index, leads, *more])

    def hop(x, shift, only=None):
        pairs = []
        for o in range(owners):
            for v in range(size):
                if only is None or only(at[v]):
                    pairs.append((o * size + v, o * size + order[(at[v] + shift) % size]))
        return lax.ppermute(x, ("occ", "vir"), pairs)

    def cross(x, rel):
        pairs = [
            (o * size + v, (o ^ rel) * size + v) for o in range(owners) for v in range(size)
        ]
        return lax.ppermute(x, ("occ", "vir"), pairs)

    def shape(dims, dtype):
        return jax.ShapeDtypeStruct(dims, dtype)

    def blocks(modes, pieces, partners, ws):
        n = len(modes) * slots
        one = shape((owners // 2, n, TILE, TILE), F32)
        product = 2 * rows * rows * width * sum_local
        keep, send = call(
            functools.partial(block_kernel, modes, pieces, owners, slots),
            (one, one),
            (meta(*partners), occ_irrep, tile_irrep),
            (t_rows, *ws),
            (pltpu.VMEM((sum_local, rows, width), BF16), pltpu.VMEM((own_rows * TILE, rows), F32)),
            flops=product * sum(2 if m == "self" else 1 for m in modes),
        )
        got = cross(send, 1)
        far = cross(keep[1] + got[1], 2)
        return keep[0] + got[0] + far

    def mirror(values, source):
        out = shape((own_rows, own_rows, TILE, TILE), BF16)
        parts = call(
            mirror_kernel,
            (out,) * owners,
            (meta(source), occ_irrep, tile_irrep),
            (values,),
        )
        return [parts[0]] + [cross(parts[q], q) for q in range(1, owners)]

    packed = call(
        pack_kernel,
        shape((cap, TILE, TILE), BF16),
        (meta(), occ_irrep, tile_irrep),
        (w_rows,),
    )
    up, down = packed, packed
    lists, mirrored = [], []
    lists.append(blocks(("self",), 1, (vir_index,), (packed,)).astype(BF16))
    for t in range(1, half):
        up, down = hop(up, 1), hop(down, -1)
        sums = blocks(("follow", "lead"), 1, (partner(-t), partner(t)), (up, down))
        other = hop(sums[:slots], -t)
        done = (sums[slots:] + other).astype(BF16)
        lists.append(done)
        mirrored += mirror(hop(done, t), partner(-t))
    cut = cap // 2
    first, second = hop(up[:cut], 1), hop(down[cut:], -1)
    sums = blocks(("either",), 2, (partner(half),), (first, second))
    other = hop(sums, half, lambda r: r >= half)
    done = (sums + other).astype(BF16)
    lists.append(done)
    mirrored += mirror(hop(done, half, lambda r: r < half), partner(half))
    partners = [partner(t) for t in range(1, half + 1)] + [partner(-t) for t in range(1, half + 1)]
    out = call(
        functools.partial(place_kernel, half, half, owners),
        shape((own_rows, occ_total, TILE, size * TILE), BF16),
        (meta(*partners), occ_irrep, tile_irrep),
        (*lists, *mirrored),
    )
    return jnp.transpose(out, (0, 2, 1, 3))


def body(owners, size, amplitudes, integrals, occ_irrep, tile_irrep):
    occ_total, vir_local, sum_local, width = amplitudes.shape
    rows = occ_total * vir_local
    t_rows = jnp.transpose(amplitudes, (2, 0, 1, 3)).reshape(sum_local, rows, width)
    w_rows = jnp.transpose(integrals, (2, 0, 1, 3)).reshape(sum_local, rows, width)
    cts = width // TILE
    ones, tiles = jnp.sum(occ_irrep), jnp.sum(tile_irrep)
    zero = (occ_total - ones) * (cts - tiles) + ones * tiles
    zero = jnp.maximum(zero, occ_total * cts - zero)
    most = jnp.maximum(ones, occ_total - ones)
    full = sum_local * occ_total * cts
    own_rows = occ_total // owners
    levels = [
        (full // 2, own_rows * occ_total // 2),
        (full // 2 + full // 16, own_rows * (occ_total // 2 + 1)),
        (full // 2 + full // 8, own_rows * (occ_total // 2 + 2)),
        (full, own_rows * occ_total),
    ]
    level = jnp.int32(len(levels) - 1)
    for n in range(len(levels) - 2, -1, -1):
        fits = (sum_local * zero <= levels[n][0]) & (own_rows * most <= levels[n][1])
        level = jnp.where(fits, n, level)
    return lax.switch(
        level,
        [functools.partial(ring_body, owners, size, cap, slots) for cap, slots in levels],
        t_rows,
        w_rows,
        occ_irrep,
        tile_irrep,
    )


def solution(mesh):
    placed = (P(None, "vir", "occ", None), P(None, "vir", "occ", None), P(), P())
    owners, size = mesh.shape["occ"], mesh.shape["vir"]

    def whole(amplitudes, integrals, occ_irrep, tile_irrep):
        one_tile = amplitudes.shape[1] == size * TILE and tile_irrep.shape[0] == size
        if one_tile and owners == 4 and size % 2 == 0:
            local = functools.partial(body, owners, size)
        else:
            local = general_body
        return jax.shard_map(
            local, mesh=mesh, in_specs=placed, out_specs=P("occ", "vir", None, None), check_vma=False
        )(amplitudes, integrals, occ_irrep, tile_irrep)

    return whole
```

```python
import functools

import jax
import jax.numpy as jnp
from jax import lax
from jax.experimental import pallas as pl
from jax.experimental.pallas import tpu as pltpu
from jax.sharding import PartitionSpec as P

TILE = 128
F32 = jnp.float32
BF16 = jnp.bfloat16
CODED = TILE + 16
VMEM_LIMIT = 48 * 1024 * 1024
SMEM_SPEC = pl.BlockSpec(memory_space=pltpu.SMEM)
VMEM_SPEC = pl.BlockSpec(memory_space=pltpu.VMEM)


def lookup(values, positions):
    hits = positions[:, None] == jnp.arange(values.shape[0], dtype=jnp.int32)[None, :]
    return jnp.sum(jnp.where(hits, values[None, :], 0), axis=1)


def pair_codes(occ_irrep, tile_irrep, occ_rows, virt_rows):
    return jnp.bitwise_xor(
        lookup(occ_irrep, occ_rows)[:, None], lookup(tile_irrep, virt_rows // TILE)[None, :]
    )


def general_body(amplitudes, integrals, occ_irrep, tile_irrep):
    occ_total, vir_local, sum_local, virt_width = amplitudes.shape
    occ_index = lax.axis_index("occ")
    vir_index = lax.axis_index("vir")
    all_occ = jnp.arange(occ_total, dtype=jnp.int32)
    all_virt = jnp.arange(virt_width, dtype=jnp.int32)
    vir_rows = vir_index * vir_local + jnp.arange(vir_local, dtype=jnp.int32)
    sum_rows = occ_index * sum_local + jnp.arange(sum_local, dtype=jnp.int32)
    left_code = pair_codes(occ_irrep, tile_irrep, all_occ, vir_rows)
    right_code = pair_codes(occ_irrep, tile_irrep, sum_rows, all_virt)
    keep = left_code[:, :, None, None] == right_code[None, None, :, :]
    amplitudes = jnp.where(keep, amplitudes, jnp.zeros_like(amplitudes))
    integrals = jnp.where(keep, integrals, jnp.zeros_like(integrals))
    flat_amplitudes = amplitudes.reshape(occ_total * vir_local, sum_local * virt_width)
    shards = lax.all_gather(integrals, "vir", axis=1, tiled=True)
    block_count = shards.shape[1]
    shard_rows = shards.reshape(occ_total * block_count, sum_local * virt_width)
    product = lax.dot_general(
        flat_amplitudes, shard_rows, (((1,), (1,)), ((), ())), preferred_element_type=jnp.float32
    )
    partial_value = product.reshape(occ_total, vir_local, occ_total, block_count)
    summed = lax.psum_scatter(partial_value, "occ", scatter_dimension=0, tiled=True)
    mirrored = lax.all_to_all(
        lax.all_to_all(summed, "vir", split_axis=3, concat_axis=1, tiled=True),
        "occ",
        split_axis=2,
        concat_axis=0,
        tiled=True,
    )
    combined = summed + jnp.transpose(mirrored, (2, 3, 0, 1))
    return combined.astype(jnp.bfloat16)


def start(size, unit):
    return pl.multiple_of(size * unit, unit)


def ring_place(vir, size):
    return jnp.where(vir % 2 == 0, vir // 2, size - 1 - vir // 2)


def vir_at(place, size):
    place = (place + size) % size
    return jnp.where(place < size // 2, 2 * place, 2 * (size - 1 - place) + 1)


class Here:
    def __init__(self, size):
        self.size = size
        self.occ = lax.axis_index("occ").astype(jnp.int32)
        self.vir = lax.axis_index("vir").astype(jnp.int32)
        self.place = ring_place(self.vir, size)
        self.leads = self.place < size // 2

    def at(self, shift):
        return vir_at(self.place + shift, self.size)


def pack_kernel(size, occ, tile, w_ref, out_ref):
    here = Here(size)
    sum_local, rows, width = w_ref.shape
    own = tile[here.vir]

    def some(m, n):
        j, k = m // sum_local, m % sum_local
        code = occ[j] ^ own ^ occ[here.occ * sum_local + k]
        for c in range(width // TILE):
            ok = (code ^ tile[c]) == 0

            @pl.when(ok)
            def _(n=n, c=c):
                out_ref[n] = w_ref[k, pl.ds(start(j, TILE), TILE), pl.ds(c * TILE, TILE)]

            n = n + ok.astype(jnp.int32)
        return n

    lax.fori_loop(0, (rows // TILE) * sum_local, some, jnp.int32(0))


def unpack(here, occ, tile, their, pieces, wd):
    sum_local, rows, width = wd.shape
    part = pieces[0].shape[0]

    def some(m, n):
        j, k = m // sum_local, m % sum_local
        code = occ[j] ^ their ^ occ[here.occ * sum_local + k]
        for c in range(width // TILE):
            ok = (code ^ tile[c]) == 0
            value = pieces[0][jnp.minimum(n, part - 1)]
            if len(pieces) == 2:
                later = pieces[1][jnp.clip(n - part, 0, part - 1)]
                value = jnp.where(n < part, value, later)
            value = jnp.where(ok, value, jnp.zeros_like(value))
            wd[k, pl.ds(start(j, TILE), TILE), pl.ds(c * TILE, TILE)] = value
            n = n + ok.astype(jnp.int32)
        return n

    lax.fori_loop(0, (rows // TILE) * sum_local, some, jnp.int32(0))


def products(a_ref, b_ref, rows):
    total = None
    for k in range(a_ref.shape[0]):
        part = lax.dot_general(
            a_ref[k], b_ref[k, rows, :], (((1,), (1,)), ((), ())), preferred_element_type=F32
        )
        total = part if total is None else total + part
    return total


def encode(ref, n, value):
    top = jnp.maximum(jnp.max(jnp.abs(value), axis=0, keepdims=True), 1e-30)
    power = jnp.ceil(jnp.log2(top)) - 14.0
    factor = jnp.ceil(top * jnp.exp2(-power))
    steps = jnp.round(value * (32767.0 / (factor * jnp.exp2(power))))
    ref[n, :TILE] = jnp.clip(steps, -32767.0, 32767.0).astype(jnp.int32).astype(jnp.int16)
    unit = jnp.concatenate(
        [jnp.broadcast_to(x, ((CODED - TILE) // 2, value.shape[1])) for x in (power, factor)]
    )
    ref[n, TILE:] = unit.astype(jnp.int32).astype(jnp.int16)


def decoded(ref, n):
    unit = ref[n, TILE:].astype(jnp.int32).astype(F32)
    power, factor = unit[:1], unit[(CODED - TILE) // 2 :][:1]
    unit = factor * jnp.exp2(power) * (1.0 / 32767.0)
    return ref[n, :TILE].astype(jnp.int32).astype(F32) * unit


def block_kernel(modes, shifts, pieces, owners, slots, size, occ, tile, t_ref, *refs):
    here = Here(size)
    count = len(modes) * pieces
    w_refs, keep_ref, send_refs, (wd, blk) = refs[:count], refs[count], refs[count + 1 : -2], refs[-2:]
    me = here.occ
    occ_total = t_ref.shape[1] // TILE
    own_rows = occ_total // owners
    wide = blk.shape[1] // TILE
    for place, mode in enumerate(modes):
        their = tile[here.at(shifts[place])]
        same = tile[here.vir] ^ their
        unpack(here, occ, tile, their, w_refs[place * pieces : (place + 1) * pieces], wd)

        def columns(step, counts, mode=mode, same=same):
            rows = pl.ds(start(step, wide * TILE), wide * TILE)
            if mode == "lead":
                blk[...] = products(t_ref, wd, rows)
            elif mode == "follow":
                blk[...] = products(wd, t_ref, rows)
            elif mode == "self":
                blk[...] = products(t_ref, wd, rows) + products(wd, t_ref, rows)
            else:

                @pl.when(here.leads)
                def _():
                    blk[...] = products(t_ref, wd, rows)

                @pl.when(jnp.logical_not(here.leads))
                def _():
                    blk[...] = products(wd, t_ref, rows)

            counts = list(counts)
            for jj in range(wide):
                code = occ[step * wide + jj] ^ same
                for q in range(owners):
                    for ii in range(own_rows):
                        i = (me ^ q) * own_rows + ii
                        ok = (occ[i] ^ code) == 0

                        @pl.when(ok)
                        def _(q=q, n=counts[q], i=i, jj=jj):
                            block = blk[pl.ds(start(i, TILE), TILE), jj * TILE : (jj + 1) * TILE]
                            if q == 0:
                                keep_ref[n] = block
                            else:
                                encode(send_refs[q - 1], n, block)

                        counts[q] = counts[q] + ok.astype(jnp.int32)
            return tuple(counts)

        first = (jnp.int32(place * slots),) * owners
        lax.fori_loop(0, occ_total // wide, columns, first)


def sum_kernel(slots, own_ref, *refs):
    count = len(refs) - 1 if slots is None else len(refs) - 1 - own_ref.shape[0] // slots
    others, sum_ref, out_refs = refs[:count], refs[count], refs[count + 1 :]

    def one(n, carry):
        total = own_ref[n]
        for other in others:
            total = total + decoded(other, n)
        sum_ref[n] = total
        for place, out_ref in enumerate(out_refs):

            @pl.when(n // slots == place)
            def _(out_ref=out_ref):
                encode(out_ref, n % slots, total)

        return carry

    lax.fori_loop(0, own_ref.shape[0], one, 0)


def mirror_kernel(shift, size, occ, tile, list_ref, codes_ref, *out_refs):
    here = Here(size)
    owners = len(out_refs)
    own_rows = out_refs[0].shape[0]
    me = here.occ
    same = tile[here.vir] ^ tile[here.at(shift)]
    last = list_ref.shape[0] - 1
    n = jnp.int32(0)
    for s in range(owners):
        for jj in range(own_rows):
            for ii in range(own_rows):
                ok = (occ[me * own_rows + ii] ^ occ[s * own_rows + jj] ^ same) == 0
                at = jnp.minimum(n, last)
                block = (list_ref[at] + decoded(codes_ref, at)).T.astype(BF16)
                block = jnp.where(ok, block, jnp.zeros_like(block))
                for q in range(owners):

                    @pl.when((s ^ me) == q)
                    def _(q=q, jj=jj, ii=ii, block=block):
                        out_refs[q][jj, ii] = block

                n = n + ok.astype(jnp.int32)


def place_kernel(half, owners, size, occ, tile, *refs):
    self_ref, out_ref = refs[0], refs[-1]
    led = refs[1 : 1 + 2 * half]
    mirrored = refs[1 + 2 * half : -1]
    own_rows, occ_total = out_ref.shape[:2]
    here = Here(size)
    me = here.occ

    def spread(partner, value):
        same = tile[here.vir] ^ tile[partner]
        cols = pl.ds(start(partner, TILE), TILE)

        def one(e, n):
            j, ii = e // own_rows, e % own_rows
            ok = (occ[me * own_rows + ii] ^ occ[j] ^ same) == 0

            @pl.when(ok)
            def _():
                out_ref[ii, j, :, cols] = value(n).astype(BF16)

            @pl.when(jnp.logical_not(ok))
            def _():
                out_ref[ii, j, :, cols] = jnp.zeros((TILE, TILE), BF16)

            return n + ok.astype(jnp.int32)

        lax.fori_loop(0, own_rows * occ_total, one, jnp.int32(0))

    def lead(t):
        list_ref, codes_ref = led[2 * (t - 1) : 2 * t]
        spread(here.at(t), lambda n: list_ref[n] + decoded(codes_ref, n))

    def lay(t):
        blocks = mirrored[(t - 1) * owners : t * owners]
        cols = pl.ds(start(here.at(-t), TILE), TILE)
        for q in range(owners):
            for jj in range(own_rows):
                for ii in range(own_rows):
                    out_ref[jj, (me ^ q) * own_rows + ii, :, cols] = blocks[q][jj, ii]

    spread(here.vir, lambda n: self_ref[n])
    for t in range(1, half):
        lead(t)
        lay(t)

    @pl.when(here.leads)
    def _():
        lead(half)

    @pl.when(jnp.logical_not(here.leads))
    def _():
        lay(half)


def call(kernel, shapes, scalars, arrays, scratch=(), flops=0):
    moved = sum(a.size * a.dtype.itemsize for a in arrays)
    return pl.pallas_call(
        kernel,
        out_shape=shapes,
        in_specs=[SMEM_SPEC] * len(scalars) + [VMEM_SPEC] * len(arrays),
        out_specs=jax.tree.map(lambda _: VMEM_SPEC, shapes),
        scratch_shapes=list(scratch),
        compiler_params=pltpu.CompilerParams(vmem_limit_bytes=VMEM_LIMIT),
        cost_estimate=pl.CostEstimate(flops=flops, bytes_accessed=2 * moved, transcendentals=0),
    )(*scalars, *arrays)


def ring_body(owners, size, cap, slots, amplitudes, w_rows, occ_irrep, tile_irrep):
    sum_local, rows, width = w_rows.shape
    occ_total = rows // TILE
    own_rows = occ_total // owners
    half = size // 2
    order = list(range(0, size, 2)) + list(range(size - 1, 0, -2))
    at = [order.index(v) for v in range(size)]
    steps = range(1, half + 1)
    scalars = (occ_irrep, tile_irrep)

    def hop(x, shift):
        pairs = [
            (o * size + v, o * size + order[(at[v] + shift) % size])
            for o in range(owners)
            for v in range(size)
        ]
        return lax.ppermute(x, ("occ", "vir"), pairs)

    def cross(x, rel):
        pairs = [
            (o * size + v, (o ^ rel) * size + v) for o in range(owners) for v in range(size)
        ]
        return lax.ppermute(x, ("occ", "vir"), pairs)

    def shape(dims, dtype):
        return jax.ShapeDtypeStruct(dims, dtype)

    def blocks(modes, shifts, pieces, ws):
        n = len(modes) * slots
        outs = (shape((n, TILE, TILE), F32),) + (shape((n, CODED, TILE), jnp.int16),) * (owners - 1)
        product = 2 * rows * rows * width * sum_local
        return call(
            functools.partial(block_kernel, modes, shifts, pieces, owners, slots, size),
            outs,
            scalars,
            (t_rows, *ws),
            (pltpu.VMEM((sum_local, rows, width), BF16), pltpu.VMEM((rows, own_rows * TILE), F32)),
            flops=product * sum(2 if m == "self" else 1 for m in modes),
        )

    def reduced(t, beside, keep, *sends):
        got = [cross(sends[q - 1], q) for q in range(1, owners)]
        keep, got = after((keep, got), beside)
        coded = shape((slots, CODED, TILE), jnp.int16)
        own = shape(keep.shape, F32)
        if t == 0:
            return call(functools.partial(sum_kernel, None), (own,), (), (keep, *got))
        lists = keep.shape[0] // slots
        return call(functools.partial(sum_kernel, slots), (own,) + (coded,) * lists, (), (keep, *got))

    def mirror(shift, values, codes):
        out = shape((own_rows, own_rows, TILE, TILE), BF16)
        parts = call(
            functools.partial(mirror_kernel, shift, size), (out,) * owners, scalars, (values, codes)
        )
        return [parts[0]] + [cross(parts[q], q) for q in range(1, owners)]

    def after(x, *others):
        return lax.optimization_barrier((x, others))[0]

    packed = call(
        functools.partial(pack_kernel, size),
        shape((cap, TILE, TILE), BF16),
        scalars,
        (w_rows,),
    )
    amplitudes = lax.optimization_barrier((amplitudes, packed))[0]
    t_rows = jnp.transpose(amplitudes, (2, 0, 1, 3)).reshape(sum_local, rows, width)
    ups, downs = [packed], [packed]
    cut = cap // 2
    raw, sums, led, mirrored = {}, {}, {}, {}

    def finish(t):
        if t == half:
            own, codes = sums[t]
            led[t] = (own, hop(codes, half))
            mirrored[t] = mirror(half, *led[t])
        else:
            own, follow, lead = sums[t]
            led[t] = (own[slots:], hop(follow, -t))
            mirrored[t] = mirror(-t, own[:slots], hop(lead, t))

    for s in range(half + 1):
        waits = raw.get(s - 1, ())
        if s + 1 < half:
            ups.append(hop(after(ups[s], waits), 1))
            downs.append(hop(after(downs[s], waits), -1))
        elif s + 1 == half:
            ups.append(hop(after(ups[s], waits)[:cut], 1))
            downs.append(hop(after(downs[s], waits)[cut:], -1))
        early = [sums.get(s - 2, ())]
        if s == 2:
            early.append(sums[1])
        if s == half:
            early.append(led[1])
        ahead_of, behind_of = after((ups[s], downs[s]), early)
        if s == 0:
            raw[0] = blocks(("self",), (0,), 1, (packed,))
        elif s < half:
            raw[s] = blocks(("follow", "lead"), (-s, s), 1, (ahead_of, behind_of))
        else:
            raw[s] = blocks(("either",), (half,), 2, (ahead_of, behind_of))
        if s in (1, half):
            sums[s] = reduced(s, (), *raw[s])
            finish(s)
        if s > 0 and s != 2:
            sums[s - 1] = reduced(s - 1, raw[s], *raw[s - 1])
            if s > 1:
                finish(s - 1)
    lists = [sums[0][0]] + [x for t in steps for x in led[t]]
    out = call(
        functools.partial(place_kernel, half, owners, size),
        shape((own_rows, occ_total, TILE, size * TILE), BF16),
        scalars,
        (*lists, *[x for t in steps for x in mirrored[t]]),
    )
    return jnp.transpose(out, (0, 2, 1, 3))


def body(owners, size, amplitudes, integrals, occ_irrep, tile_irrep):
    occ_total, vir_local, sum_local, width = amplitudes.shape
    rows = occ_total * vir_local
    w_rows = jnp.transpose(integrals, (2, 0, 1, 3)).reshape(sum_local, rows, width)
    cts = width // TILE
    ones, tiles = jnp.sum(occ_irrep), jnp.sum(tile_irrep)
    zero = (occ_total - ones) * (cts - tiles) + ones * tiles
    zero = jnp.maximum(zero, occ_total * cts - zero)
    most = jnp.maximum(ones, occ_total - ones)
    full = sum_local * occ_total * cts
    own_rows = occ_total // owners
    levels = [
        (full, own_rows * occ_total),
        (full // 2 + full // 8, own_rows * (occ_total // 2 + 2)),
        (full // 2, own_rows * occ_total // 2),
        (full // 2 + full // 16, own_rows * (occ_total // 2 + 1)),
    ]
    level = jnp.int32(0)
    for n in (1, 3, 2):
        fits = (sum_local * zero <= levels[n][0]) & (own_rows * most <= levels[n][1])
        level = jnp.where(fits, n, level)
    return lax.switch(
        level,
        [functools.partial(ring_body, owners, size, cap, slots) for cap, slots in levels],
        amplitudes,
        w_rows,
        occ_irrep,
        tile_irrep,
    )


def solution(mesh):
    placed = (P(None, "vir", "occ", None), P(None, "vir", "occ", None), P(), P())
    owners, size = mesh.shape["occ"], mesh.shape["vir"]

    def whole(amplitudes, integrals, occ_irrep, tile_irrep):
        one_tile = amplitudes.shape[1] == size * TILE and tile_irrep.shape[0] == size
        if one_tile and owners == 4 and size % 2 == 0:
            local = functools.partial(body, owners, size)
        else:
            local = general_body
        return jax.shard_map(
            local, mesh=mesh, in_specs=placed, out_specs=P("occ", "vir", None, None), check_vma=False
        )(amplitudes, integrals, occ_irrep, tile_irrep)

    return whole
```

```python
import functools

import jax
import jax.numpy as jnp
from jax import lax
from jax.experimental import pallas as pl
from jax.experimental.pallas import tpu as pltpu
from jax.sharding import PartitionSpec as P

TILE = 128
F32 = jnp.float32
BF16 = jnp.bfloat16
CODED = TILE + 16
VMEM_LIMIT = 48 * 1024 * 1024
SMEM_SPEC = pl.BlockSpec(memory_space=pltpu.SMEM)
VMEM_SPEC = pl.BlockSpec(memory_space=pltpu.VMEM)


def lookup(values, positions):
    hits = positions[:, None] == jnp.arange(values.shape[0], dtype=jnp.int32)[None, :]
    return jnp.sum(jnp.where(hits, values[None, :], 0), axis=1)


def pair_codes(occ_irrep, tile_irrep, occ_rows, virt_rows):
    return jnp.bitwise_xor(
        lookup(occ_irrep, occ_rows)[:, None], lookup(tile_irrep, virt_rows // TILE)[None, :]
    )


def general_body(amplitudes, integrals, occ_irrep, tile_irrep):
    occ_total, vir_local, sum_local, virt_width = amplitudes.shape
    occ_index = lax.axis_index("occ")
    vir_index = lax.axis_index("vir")
    all_occ = jnp.arange(occ_total, dtype=jnp.int32)
    all_virt = jnp.arange(virt_width, dtype=jnp.int32)
    vir_rows = vir_index * vir_local + jnp.arange(vir_local, dtype=jnp.int32)
    sum_rows = occ_index * sum_local + jnp.arange(sum_local, dtype=jnp.int32)
    left_code = pair_codes(occ_irrep, tile_irrep, all_occ, vir_rows)
    right_code = pair_codes(occ_irrep, tile_irrep, sum_rows, all_virt)
    keep = left_code[:, :, None, None] == right_code[None, None, :, :]
    amplitudes = jnp.where(keep, amplitudes, jnp.zeros_like(amplitudes))
    integrals = jnp.where(keep, integrals, jnp.zeros_like(integrals))
    flat_amplitudes = amplitudes.reshape(occ_total * vir_local, sum_local * virt_width)
    shards = lax.all_gather(integrals, "vir", axis=1, tiled=True)
    block_count = shards.shape[1]
    shard_rows = shards.reshape(occ_total * block_count, sum_local * virt_width)
    product = lax.dot_general(
        flat_amplitudes, shard_rows, (((1,), (1,)), ((), ())), preferred_element_type=jnp.float32
    )
    partial_value = product.reshape(occ_total, vir_local, occ_total, block_count)
    summed = lax.psum_scatter(partial_value, "occ", scatter_dimension=0, tiled=True)
    mirrored = lax.all_to_all(
        lax.all_to_all(summed, "vir", split_axis=3, concat_axis=1, tiled=True),
        "occ",
        split_axis=2,
        concat_axis=0,
        tiled=True,
    )
    combined = summed + jnp.transpose(mirrored, (2, 3, 0, 1))
    return combined.astype(jnp.bfloat16)


def start(size, unit):
    return pl.multiple_of(size * unit, unit)


def ring_place(vir, size):
    return jnp.where(vir % 2 == 0, vir // 2, size - 1 - vir // 2)


def vir_at(place, size):
    place = (place + size) % size
    return jnp.where(place < size // 2, 2 * place, 2 * (size - 1 - place) + 1)


class Here:
    def __init__(self, size):
        self.size = size
        self.occ = lax.axis_index("occ").astype(jnp.int32)
        self.vir = lax.axis_index("vir").astype(jnp.int32)
        self.place = ring_place(self.vir, size)
        self.leads = self.place < size // 2

    def at(self, shift):
        return vir_at(self.place + shift, self.size)


def pack_kernel(size, occ, tile, w_ref, out_ref):
    here = Here(size)
    sum_local, rows, width = w_ref.shape
    own = tile[here.vir]

    def some(m, n):
        j, k = m // sum_local, m % sum_local
        code = occ[j] ^ own ^ occ[here.occ * sum_local + k]
        for c in range(width // TILE):
            ok = (code ^ tile[c]) == 0

            @pl.when(ok)
            def _(n=n, c=c):
                out_ref[n] = w_ref[k, pl.ds(start(j, TILE), TILE), pl.ds(c * TILE, TILE)]

            n = n + ok.astype(jnp.int32)
        return n

    lax.fori_loop(0, (rows // TILE) * sum_local, some, jnp.int32(0))


def unpack(here, occ, tile, their, pieces, wd):
    sum_local, rows, width = wd.shape
    part = pieces[0].shape[0]

    def some(m, n):
        j, k = m // sum_local, m % sum_local
        code = occ[j] ^ their ^ occ[here.occ * sum_local + k]
        for c in range(width // TILE):
            ok = (code ^ tile[c]) == 0
            value = pieces[0][jnp.minimum(n, part - 1)]
            if len(pieces) == 2:
                later = pieces[1][jnp.clip(n - part, 0, part - 1)]
                value = jnp.where(n < part, value, later)
            value = jnp.where(ok, value, jnp.zeros_like(value))
            wd[k, pl.ds(start(j, TILE), TILE), pl.ds(c * TILE, TILE)] = value
            n = n + ok.astype(jnp.int32)
        return n

    lax.fori_loop(0, (rows // TILE) * sum_local, some, jnp.int32(0))


def multiply(blk, first, a_ref, b_ref, rows):
    part = blk.shape[0] // 2

    def some(m, carry):
        at = pl.ds(start(m, part), part)
        total = None if first else blk[at, :]
        for k in range(a_ref.shape[0]):
            more = lax.dot_general(
                a_ref[k, at, :], b_ref[k, rows, :], (((1,), (1,)), ((), ())), preferred_element_type=F32
            )
            total = more if total is None else total + more
        blk[at, :] = total
        return carry

    lax.fori_loop(0, 2, some, 0)


def encode(ref, n, value):
    top = jnp.maximum(jnp.max(jnp.abs(value), axis=0, keepdims=True), 1e-30)
    power = jnp.ceil(jnp.log2(top)) - 14.0
    factor = jnp.ceil(top * jnp.exp2(-power))
    steps = jnp.round(value * (32767.0 / (factor * jnp.exp2(power))))
    ref[n, :TILE] = jnp.clip(steps, -32767.0, 32767.0).astype(jnp.int32).astype(jnp.int16)
    unit = jnp.concatenate(
        [jnp.broadcast_to(x, ((CODED - TILE) // 2, value.shape[1])) for x in (power, factor)]
    )
    ref[n, TILE:] = unit.astype(jnp.int32).astype(jnp.int16)


def decoded(ref, n):
    unit = ref[n, TILE:].astype(jnp.int32).astype(F32)
    power, factor = unit[:1], unit[(CODED - TILE) // 2 :][:1]
    unit = factor * jnp.exp2(power) * (1.0 / 32767.0)
    return ref[n, :TILE].astype(jnp.int32).astype(F32) * unit


def block_kernel(modes, shifts, pieces, owners, slots, size, occ, tile, t_ref, *refs):
    here = Here(size)
    count = len(modes) * pieces
    w_refs, keep_ref, send_refs, (wd, blk, raw) = refs[:count], refs[count], refs[count + 1 : -3], refs[-3:]
    me = here.occ
    occ_total = t_ref.shape[1] // TILE
    own_rows = occ_total // owners
    wide = blk.shape[1] // TILE
    for place, mode in enumerate(modes):
        their = tile[here.at(shifts[place])]
        same = tile[here.vir] ^ their
        unpack(here, occ, tile, their, w_refs[place * pieces : (place + 1) * pieces], wd)

        def columns(step, counts, mode=mode, same=same, place=place):
            rows = pl.ds(start(step, wide * TILE), wide * TILE)
            if mode == "lead":
                multiply(blk, True, t_ref, wd, rows)
            elif mode == "follow":
                multiply(blk, True, wd, t_ref, rows)
            elif mode == "self":
                multiply(blk, True, t_ref, wd, rows)
                multiply(blk, False, wd, t_ref, rows)
            else:

                @pl.when(here.leads)
                def _():
                    multiply(blk, True, t_ref, wd, rows)

                @pl.when(jnp.logical_not(here.leads))
                def _():
                    multiply(blk, True, wd, t_ref, rows)

            counts = list(counts)
            for jj in range(wide):
                code = occ[step * wide + jj] ^ same
                for q in range(owners):
                    for ii in range(own_rows):
                        i = (me ^ q) * own_rows + ii
                        ok = (occ[i] ^ code) == 0

                        @pl.when(ok)
                        def _(q=q, n=counts[q], i=i, jj=jj):
                            block = blk[pl.ds(start(i, TILE), TILE), jj * TILE : (jj + 1) * TILE]
                            if q == 0:
                                keep_ref[place * slots + n] = block
                            else:
                                raw[q - 1, n] = block

                        counts[q] = counts[q] + ok.astype(jnp.int32)
            return tuple(counts)

        counts = lax.fori_loop(0, occ_total // wide, columns, (jnp.int32(0),) * owners)
        for q in range(1, owners):

            def coded(n, carry, q=q, place=place):
                encode(send_refs[q - 1], place * slots + n, raw[q - 1, n])
                return carry

            lax.fori_loop(0, counts[q], coded, 0)


def sum_kernel(slots, own_ref, *refs):
    count = len(refs) - 1 if slots is None else len(refs) - 1 - own_ref.shape[0] // slots
    others, sum_ref, out_refs = refs[:count], refs[count], refs[count + 1 :]

    def one(n, carry):
        total = own_ref[n]
        for other in others:
            total = total + decoded(other, n)
        sum_ref[n] = total
        for place, out_ref in enumerate(out_refs):

            @pl.when(n // slots == place)
            def _(out_ref=out_ref):
                encode(out_ref, n % slots, total)

        return carry

    lax.fori_loop(0, own_ref.shape[0], one, 0)


def mirror_kernel(shift, size, occ, tile, list_ref, codes_ref, *out_refs):
    here = Here(size)
    owners = len(out_refs)
    own_rows = out_refs[0].shape[0]
    me = here.occ
    same = tile[here.vir] ^ tile[here.at(shift)]
    last = list_ref.shape[0] - 1

    def one(e, n):
        j, ii = e // own_rows, e % own_rows
        ok = (occ[me * own_rows + ii] ^ occ[j] ^ same) == 0
        at = jnp.minimum(n, last)
        block = (list_ref[at] + decoded(codes_ref, at)).T.astype(BF16)
        block = jnp.where(ok, block, jnp.zeros_like(block))
        for q in range(owners):

            @pl.when((j // own_rows) ^ me == q)
            def _(q=q):
                out_refs[q][j % own_rows, ii] = block

        return n + ok.astype(jnp.int32)

    lax.fori_loop(0, own_rows * own_rows * owners, one, jnp.int32(0))


def place_kernel(half, owners, size, occ, tile, *refs):
    self_ref, out_ref = refs[0], refs[-1]
    led = refs[1 : 1 + 2 * half]
    mirrored = refs[1 + 2 * half : -1]
    own_rows, occ_total = out_ref.shape[:2]
    here = Here(size)
    me = here.occ

    def spread(partner, value):
        same = tile[here.vir] ^ tile[partner]
        cols = pl.ds(start(partner, TILE), TILE)

        def one(e, n):
            j, ii = e // own_rows, e % own_rows
            ok = (occ[me * own_rows + ii] ^ occ[j] ^ same) == 0

            @pl.when(ok)
            def _():
                out_ref[ii, j, :, cols] = value(n).astype(BF16)

            @pl.when(jnp.logical_not(ok))
            def _():
                out_ref[ii, j, :, cols] = jnp.zeros((TILE, TILE), BF16)

            return n + ok.astype(jnp.int32)

        lax.fori_loop(0, own_rows * occ_total, one, jnp.int32(0))

    def lead(t):
        list_ref, codes_ref = led[2 * (t - 1) : 2 * t]
        spread(here.at(t), lambda n: list_ref[n] + decoded(codes_ref, n))

    def lay(t):
        blocks = mirrored[(t - 1) * owners : t * owners]
        cols = pl.ds(start(here.at(-t), TILE), TILE)
        for q in range(owners):

            def one(e, carry, q=q):
                jj, ii = e // own_rows, e % own_rows
                out_ref[jj, (me ^ q) * own_rows + ii, :, cols] = blocks[q][jj, ii]
                return carry

            lax.fori_loop(0, own_rows * own_rows, one, 0)

    spread(here.vir, lambda n: self_ref[n])
    for t in range(1, half):
        lead(t)
        lay(t)

    @pl.when(here.leads)
    def _():
        lead(half)

    @pl.when(jnp.logical_not(here.leads))
    def _():
        lay(half)


def call(kernel, shapes, scalars, arrays, scratch=(), flops=0):
    moved = sum(a.size * a.dtype.itemsize for a in arrays)
    return pl.pallas_call(
        kernel,
        out_shape=shapes,
        in_specs=[SMEM_SPEC] * len(scalars) + [VMEM_SPEC] * len(arrays),
        out_specs=jax.tree.map(lambda _: VMEM_SPEC, shapes),
        scratch_shapes=list(scratch),
        compiler_params=pltpu.CompilerParams(vmem_limit_bytes=VMEM_LIMIT),
        cost_estimate=pl.CostEstimate(flops=flops, bytes_accessed=2 * moved, transcendentals=0),
    )(*scalars, *arrays)


def ring_body(owners, size, cap, slots, amplitudes, w_rows, occ_irrep, tile_irrep):
    sum_local, rows, width = w_rows.shape
    occ_total = rows // TILE
    own_rows = occ_total // owners
    half = size // 2
    order = list(range(0, size, 2)) + list(range(size - 1, 0, -2))
    at = [order.index(v) for v in range(size)]
    steps = range(1, half + 1)
    scalars = (occ_irrep, tile_irrep)

    def hop(x, shift):
        pairs = [
            (o * size + v, o * size + order[(at[v] + shift) % size])
            for o in range(owners)
            for v in range(size)
        ]
        return lax.ppermute(x, ("occ", "vir"), pairs)

    def cross(x, rel):
        pairs = [
            (o * size + v, (o ^ rel) * size + v) for o in range(owners) for v in range(size)
        ]
        return lax.ppermute(x, ("occ", "vir"), pairs)

    def shape(dims, dtype):
        return jax.ShapeDtypeStruct(dims, dtype)

    def blocks(modes, shifts, pieces, ws):
        n = len(modes) * slots
        outs = (shape((n, TILE, TILE), F32),) + (shape((n, CODED, TILE), jnp.int16),) * (owners - 1)
        product = 2 * rows * rows * width * sum_local
        return call(
            functools.partial(block_kernel, modes, shifts, pieces, owners, slots, size),
            outs,
            scalars,
            (t_rows, *ws),
            (
                pltpu.VMEM((sum_local, rows, width), BF16),
                pltpu.VMEM((rows, own_rows * TILE), F32),
                pltpu.VMEM((owners - 1, slots, TILE, TILE), F32),
            ),
            flops=product * sum(2 if m == "self" else 1 for m in modes),
        )

    def reduced(t, beside, keep, *sends):
        got = [cross(sends[q - 1], q) for q in range(1, owners)]
        keep, got = after((keep, got), beside)
        coded = shape((slots, CODED, TILE), jnp.int16)
        own = shape(keep.shape, F32)
        if t == 0:
            return call(functools.partial(sum_kernel, None), (own,), (), (keep, *got))
        return call(functools.partial(sum_kernel, slots), (own, coded), (), (keep, *got))

    def mirror(shift, values, codes):
        out = shape((own_rows, own_rows, TILE, TILE), BF16)
        parts = call(
            functools.partial(mirror_kernel, shift, size), (out,) * owners, scalars, (values, codes)
        )
        return [parts[0]] + [cross(parts[q], q) for q in range(1, owners)]

    def after(x, *others):
        return lax.optimization_barrier((x, others))[0]

    packed = call(
        functools.partial(pack_kernel, size),
        shape((cap, TILE, TILE), BF16),
        scalars,
        (w_rows,),
    )
    amplitudes = lax.optimization_barrier((amplitudes, packed))[0]
    t_rows = jnp.transpose(amplitudes, (2, 0, 1, 3)).reshape(sum_local, rows, width)
    ups, downs = [packed], [packed]
    cut = cap // 2
    raw, sums, led, mirrored = {}, {}, {}, {}

    def finish(t):
        if t == half:
            own, codes = sums[t]
            led[t] = (own, hop(codes, half))
            mirrored[t] = mirror(half, *led[t])
        else:
            (own, follow), (lead_own, lead) = sums[t]
            led[t] = (lead_own, hop(follow, -t))
            mirrored[t] = mirror(-t, own, hop(lead, t))

    for s in range(half + 1):
        waits = sums.get(s - 1, ())
        if s + 1 < half:
            ups.append(hop(after(ups[s], waits), 1))
            downs.append(hop(after(downs[s], waits), -1))
        elif s + 1 == half:
            ups.append(hop(after(ups[s], waits)[:cut], 1))
            downs.append(hop(after(downs[s], waits)[cut:], -1))
        early = led[1] if s == half else ()
        ahead_of, behind_of = after((ups[s], downs[s]), early)
        if s == 0:
            raw[0] = blocks(("self",), (0,), 1, (packed,))
        elif s < half:
            raw[s] = (
                blocks(("follow",), (-s,), 1, (ahead_of,)),
                blocks(("lead",), (s,), 1, (behind_of,)),
            )
        else:
            raw[s] = blocks(("either",), (half,), 2, (ahead_of, behind_of))
        if s in (0, half):
            sums[s] = reduced(s, (), *raw[s])
        elif s < half - 1:
            sums[s] = tuple(reduced(s, (), *one) for one in raw[s])
        if s == half:
            sums[s - 1] = tuple(reduced(s - 1, raw[s], *one) for one in raw[s - 1])
            finish(s - 1)
        if s not in (0, half - 1):
            finish(s)
    lists = [sums[0][0]] + [x for t in steps for x in led[t]]
    out = call(
        functools.partial(place_kernel, half, owners, size),
        shape((own_rows, occ_total, TILE, size * TILE), BF16),
        scalars,
        (*lists, *[x for t in steps for x in mirrored[t]]),
    )
    return jnp.transpose(out, (0, 2, 1, 3))


def body(owners, size, amplitudes, integrals, occ_irrep, tile_irrep):
    occ_total, vir_local, sum_local, width = amplitudes.shape
    rows = occ_total * vir_local
    w_rows = jnp.transpose(integrals, (2, 0, 1, 3)).reshape(sum_local, rows, width)
    cts = width // TILE
    ones, tiles = jnp.sum(occ_irrep), jnp.sum(tile_irrep)
    zero = (occ_total - ones) * (cts - tiles) + ones * tiles
    zero = jnp.maximum(zero, occ_total * cts - zero)
    most = jnp.maximum(ones, occ_total - ones)
    full = sum_local * occ_total * cts
    own_rows = occ_total // owners
    levels = [
        (full, own_rows * occ_total),
        (full // 2 + full // 8, own_rows * (occ_total // 2 + 2)),
        (full // 2, own_rows * occ_total // 2),
        (full // 2 + full // 16, own_rows * (occ_total // 2 + 1)),
    ]
    level = jnp.int32(0)
    for n in (1, 3, 2):
        fits = (sum_local * zero <= levels[n][0]) & (own_rows * most <= levels[n][1])
        level = jnp.where(fits, n, level)
    return lax.switch(
        level,
        [functools.partial(ring_body, owners, size, cap, slots) for cap, slots in levels],
        amplitudes,
        w_rows,
        occ_irrep,
        tile_irrep,
    )


def solution(mesh):
    placed = (P(None, "vir", "occ", None), P(None, "vir", "occ", None), P(), P())
    owners, size = mesh.shape["occ"], mesh.shape["vir"]

    def whole(amplitudes, integrals, occ_irrep, tile_irrep):
        one_tile = amplitudes.shape[1] == size * TILE and tile_irrep.shape[0] == size
        if one_tile and owners == 4 and size % 2 == 0:
            local = functools.partial(body, owners, size)
        else:
            local = general_body
        return jax.shard_map(
            local, mesh=mesh, in_specs=placed, out_specs=P("occ", "vir", None, None), check_vma=False
        )(amplitudes, integrals, occ_irrep, tile_irrep)

    return whole
```
